32 devices in a mesh: row: 16 (over z, y, core), loop: 2 (over x).
Axes of the slice: x: 2, y: 2, z: 4, core: 2. Of those that a mesh axis runs over, the one named last changes fastest.
Arguments:
- panels: float32 [512, 256], P('loop'), may hold values from -0.3 to 0.3
- right_side: float32 [32768, 256], P(('row', 'loop')), may hold values from -6 to 6
- block_users: int32 [768], P(('row', 'loop')), may hold values from 0 to 7
- block_items: int32 [768], P(('row', 'loop')), may hold values from 0 to 1
- masks: int32 [768, 128, 128], P(('row', 'loop')), may hold values 0 or 1
- self_tiles: float32 [32768, 128], P(('row', 'loop')), may hold values from 0 to 0.02
- next_tiles: float32 [32768, 128], P(('row', 'loop')), may hold values from 0 to 0.02
Outputs:
- solution_field: float32 [32768, 256], P(('row', 'loop'))
- residual: float32 [32768, 256], P(('row', 'loop'))
The draws below stay inside these ranges and needn't reach their ends.
All inputs are finite; a program needn't handle non-finite values. No bound on the sum of `masks` on one device may be relied on, other than what follows from the above.
Results may differ from the reference program's by a relative error of at most 0.00045.
Values sent between devices are 32-bit elements; how exact they have to be, the bound alone decides.
A program may use at most 64 MiB of HBM per device.

```python
import jax
import jax.numpy as jnp
from jax import lax

K = 256
BLK = 128
ITERS = 2
UB_DEV = 8
PANEL_BLOCKS = 2
PER_PANEL = 12
NB_DEV = 24
USERS = 32768
ITEMS = 512
N_LOOP = 2
DEVICES = 32


def set_ends(drawn, rng, smallest, largest):
    dims = drawn.shape
    index_at = [jax.random.randint(jax.random.fold_in(rng, axis), (), 0, dims[axis]) for axis in range(len(dims))]
    drawn = drawn.at[tuple(index_at)].set(smallest)
    longest = dims.index(max(dims))
    index_at[longest] = (index_at[longest] + 1) % dims[longest]
    return drawn.at[tuple(index_at)].set(largest)


def levels(rng, dims, pieces, least, top_value):
    loudness = 1.0
    for position, blocks in pieces:
        heights = jax.random.uniform(jax.random.fold_in(jax.random.fold_in(rng, 6), position), (blocks,), jnp.float32, least / len(pieces), top_value / len(pieces))
        loudness = loudness * jnp.repeat(jnp.exp(heights), dims[position] // blocks).reshape((-1,) + (1,) * (len(dims) - 1 - position))
    return loudness


def gaussian(rng, extent, scale, reach, shards=(), held_as=jnp.bfloat16):
    factor_of = levels(rng, extent, shards, -0.22, 0.18) if shards else 1.0
    values = jax.random.normal(rng, extent, jnp.float32) * scale * factor_of
    return jnp.minimum(jnp.maximum(values, -reach), reach).astype(held_as)


def setup_inputs(seed: int = 0) -> dict:
    seeds = jax.random.split(jax.random.key(seed), 8)
    panels = gaussian(seeds[0], (ITEMS, K), 0.05, 0.3, ((0, 2),), jnp.float32)
    right_side = gaussian(seeds[1], (USERS, K), 1.0, 6.0, ((0, 32),), jnp.float32)
    block_users = set_ends(jax.random.randint(seeds[2], (NB_DEV * DEVICES,), 0, UB_DEV), jax.random.fold_in(seeds[2], 1), 0, UB_DEV - 1).astype(jnp.int32)
    block_items = set_ends(jax.random.randint(seeds[3], (NB_DEV * DEVICES,), 0, PANEL_BLOCKS), jax.random.fold_in(seeds[3], 1), 0, PANEL_BLOCKS - 1).astype(jnp.int32)
    masks = set_ends((jax.random.randint(seeds[4], (NB_DEV * DEVICES, BLK, BLK), 0, 2) < 1).astype(jnp.int32), jax.random.fold_in(seeds[4], 1), 0, 1)
    self_tiles = jnp.clip(0.02 * jax.random.uniform(seeds[5], (USERS, BLK), jnp.float32) ** levels(seeds[5], (USERS, BLK), ((0, 32),), -0.2, 0.2), 0.0, 0.02)
    next_tiles = jnp.clip(0.02 * jax.random.uniform(seeds[6], (USERS, BLK), jnp.float32) ** levels(seeds[6], (USERS, BLK), ((0, 32),), -0.2, 0.2), 0.0, 0.02)
    return {"panels": panels, "right_side": right_side, "block_users": block_users, "block_items": block_items, "masks": masks, "self_tiles": self_tiles, "next_tiles": next_tiles}


ridge_weight = 0.5
highest = lax.Precision.HIGHEST


def gram_apply(direction, panels, block_users, block_items, masks):
    device_count = USERS // (UB_DEV * BLK)
    list_length = PER_PANEL * N_LOOP
    user_tiles = direction.reshape(-1, BLK, K)
    item_tiles = panels.reshape(-1, BLK, K)
    offsets = jnp.arange(device_count, dtype=jnp.int32) * UB_DEV
    user_list = block_users.reshape(device_count, list_length).astype(jnp.int32) + offsets[:, None]
    panel_of = jnp.arange(list_length, dtype=jnp.int32) // PER_PANEL
    item_list = block_items.reshape(device_count, list_length).astype(jnp.int32) + panel_of[None, :] * PANEL_BLOCKS
    mask_list = masks.reshape(device_count, list_length, BLK, BLK)

    def visit_device(summed, inputs):
        user_ids, item_ids, mask_tiles = inputs
        left_tiles = user_tiles[user_ids]
        right_tiles = item_tiles[item_ids]
        scores = jnp.einsum("bik,bjk->bij", left_tiles, right_tiles, precision=highest) * mask_tiles.astype(left_tiles.dtype)
        contrib = jnp.einsum("bij,bjk->bik", scores, right_tiles, precision=highest)
        return summed.at[user_ids].add(contrib), None

    summed = lax.scan(visit_device, jnp.zeros_like(user_tiles), (user_list, item_list, mask_list))[0]
    return summed.reshape(-1, K)


def graph_apply(field_in, self_tiles, next_tiles):
    own_tiles = self_tiles.reshape(-1, BLK, BLK)
    symmetric = 0.5 * (own_tiles + jnp.swapaxes(own_tiles, 1, 2))
    onward = next_tiles.reshape(-1, BLK, BLK)
    blocks = field_in.reshape(-1, BLK, K)
    zero_block = jnp.zeros_like(blocks[:1])
    following = jnp.concatenate([blocks[1:], zero_block], axis=0)
    backward = jnp.einsum("bji,bjk->bik", onward[:-1], blocks[:-1], precision=highest)
    preceding = jnp.concatenate([zero_block, backward], axis=0)
    coupled = jnp.einsum("bij,bjk->bik", symmetric, blocks, precision=highest)
    coupled = coupled + jnp.einsum("bij,bjk->bik", onward, following, precision=highest) + preceding
    column_sums = jnp.sum(onward[:-1], axis=1)
    degree = jnp.sum(symmetric, axis=2) + jnp.sum(onward, axis=2)
    degree = degree + jnp.concatenate([jnp.zeros((1, BLK), onward.dtype), column_sums], axis=0)
    return degree.reshape(-1), coupled.reshape(-1, K)


def reference(panels, right_side, block_users, block_items, masks, self_tiles, next_tiles):
    def operate(direction):
        degree, coupled = graph_apply(direction, self_tiles, next_tiles)
        gram_part = gram_apply(direction, panels, block_users, block_items, masks)
        return gram_part + (ridge_weight + degree)[:, None] * direction - coupled

    solution_field = jnp.zeros_like(right_side)
    residual = right_side
    direction = right_side
    norm_now = jnp.sum(residual * residual)
    for turn_index in range(ITERS):
        image = operate(direction)
        step_size = norm_now / jnp.sum(direction * image)
        solution_field = solution_field + step_size * direction
        residual = residual - step_size * image
        norm_next = jnp.sum(residual * residual)
        direction = residual + (norm_next / norm_now) * direction
        norm_now = norm_next
    return solution_field, residual
```

```python
import functools

import jax
import jax.numpy as jnp
from jax import lax
from jax.experimental import pallas as pl
from jax.experimental.pallas import tpu as pltpu
from jax.sharding import PartitionSpec as P

ridge_weight = 0.5
MESH = pl.DeviceIdType.MESH
F32 = jnp.float32
BF16 = jnp.bfloat16
COUNT_BITS = 4
NN = (((1,), (0,)), ((), ()))
NT = (((1,), (1,)), ((), ()))
TN = (((0,), (0,)), ((), ()))


def halves(x):
    high = x.astype(BF16)
    return high, (x - high.astype(F32)).astype(BF16)


def dot3(a, b, dims):
    dot = functools.partial(lax.dot_general, dimension_numbers=dims, preferred_element_type=F32)
    return dot(a[0], b[0]) + (dot(a[1], b[0]) + dot(a[0], b[1]))


def lanes(x):
    rows, width = x.shape
    x = sum(x[:, c : c + 128] for c in range(0, width, 128))
    return jnp.sum(x, axis=0, keepdims=True)


def kernel(
    sizes,
    users_ref,
    items_ref,
    panel_ref,
    right_ref,
    mask_ref,
    self_ref,
    next_ref,
    q_out,
    p_out,
    coef_out,
    b_v,
    q_v,
    p_v,
    v_hi,
    v_lo,
    panel_v,
    h_hi,
    h_lo,
    mask_v,
    packed,
    self_v,
    next_v,
    w_hi,
    w_lo,
    diag,
    ahead,
    carried,
    product,
    columns_out,
    columns_in,
    mine,
    near,
    near_sum,
    far,
    local_sem,
    panel_s,
    panel_r,
    share_s,
    share_r,
    halo_s,
    halo_r,
    near_s,
    near_r,
    far_s,
    far_r,
):
    R, L, g, T, U, K, PR, per_panel = sizes
    Z = R // g
    G = g * L
    row, loop = lax.axis_index("row"), lax.axis_index("loop")
    n = R * L
    d = row * L + loop
    me_near = lax.rem(row, g) * L + loop
    me_far = row // g
    quarter = lax.rem(row, g)
    base = me_far * g
    after, before = lax.rem(d + 1, n), lax.rem(d + n - 1, n)
    after = (after // L, lax.rem(after, L))
    before = (before // L, lax.rem(before, L))
    has_after, has_before = d < n - 1, d > 0
    tail = (U - 1) * T

    loads = [
        pltpu.make_async_copy(src, dst, local_sem.at[i])
        for i, (src, dst) in enumerate(
            [
                (next_ref, next_v),
                (right_ref, b_v),
                (self_ref, self_v),
                (panel_ref, panel_v.at[0]),
                (mask_ref, mask_v),
            ]
        )
    ]
    for load in loads:
        load.start()

    def near_device(i):
        t = lax.rem(me_near + i, G)
        return t, (base + t // L, lax.rem(t, L))

    def far_device(i):
        t = lax.rem(me_far + i, Z)
        return t, (t * g + quarter, loop)

    barrier = pltpu.get_barrier_semaphore()
    greeted = [near_device(i)[1] for i in range(1, G)] + [far_device(i)[1] for i in range(1, Z)]
    greeted += [after, before]
    for device in greeted:
        pl.semaphore_signal(barrier, inc=1, device_id=device, device_id_type=MESH)
    pl.semaphore_wait(barrier, len(greeted))

    def remote(src, dst, send, recv, device):
        return pltpu.make_async_remote_copy(
            src_ref=src, dst_ref=dst, send_sem=send, recv_sem=recv, device_id=device, device_id_type=MESH
        )

    part = PR // g

    def share(k, which):
        return panel_v.at[k, pl.ds(pl.multiple_of(which * part, part), part)]

    own_share = panel_ref.at[pl.ds(pl.multiple_of(quarter * part, part), part)]
    direct = [
        remote(own_share, share(k, quarter), panel_s.at[k], panel_r.at[k], (row, lax.rem(loop + L - k, L)))
        for k in range(1, L)
    ]
    for copy in direct:
        copy.start()

    def forwards(k):
        copies = []
        for i in range(1, g):
            t = lax.rem(quarter + i, g)
            copies.append(
                remote(share(k, quarter), share(k, quarter), share_s.at[k, i], share_r.at[k, quarter], (base + t, loop))
            )
        return copies

    def forward_in(k, i):
        t = lax.rem(quarter + i, g)
        return remote(share(k, t), share(k, t), share_s.at[k, i], share_r.at[k, t], (base + t, loop))

    first_0 = remote(right_ref.at[pl.ds(0, T)], ahead.at[0], halo_s.at[0, 0], halo_r.at[0, 0], before)
    first_1 = remote(q_v.at[pl.ds(0, T)], ahead.at[1], halo_s.at[1, 0], halo_r.at[1, 0], before)
    product_copies = [
        remote(product.at[ph], carried.at[ph], halo_s.at[ph, 1], halo_r.at[ph, 1], after) for ph in range(2)
    ]
    columns_copy = remote(columns_out, columns_in, halo_s.at[0, 2], halo_r.at[0, 2], after)

    @pl.when(has_before)
    def _():
        first_0.start()

    @pl.when(jnp.logical_not(has_before))
    def _():
        carried[...] = jnp.zeros_like(carried)
        columns_in[...] = jnp.zeros_like(columns_in)

    @pl.when(jnp.logical_not(has_after))
    def _():
        ahead[...] = jnp.zeros_like(ahead)

    loads[0].wait()
    loads[1].wait()
    last_next = next_v[tail:]
    columns_out[...] = jnp.broadcast_to(jnp.sum(last_next, axis=0, keepdims=True), columns_out.shape)
    last_turned = halves(last_next.T)
    product[0] = dot3(last_turned, halves(b_v[tail:]), NN)

    @pl.when(has_after)
    def _():
        columns_copy.start()
        product_copies[0].start()

    loads[2].wait()
    degrees = []
    onward_columns = None
    for b in range(U):
        rows = slice(b * T, (b + 1) * T)
        own = self_v[rows]
        sym = 0.5 * (own + own.T)
        onward = next_v[rows]
        turned = onward.T
        degree = jnp.sum(sym, axis=1, keepdims=True) + jnp.sum(onward, axis=1, keepdims=True)
        if onward_columns is not None:
            degree = degree + onward_columns
        onward_columns = jnp.sum(turned, axis=1, keepdims=True)
        diag[rows] = jnp.broadcast_to(degree + ridge_weight, (T, T))
        for place, tile, target in ((1, sym, b), (2, onward, b), (0, turned, b + 1)):
            if target < U:
                high, low = halves(tile)
                w_hi[target, :, place * T : (place + 1) * T] = high
                w_lo[target, :, place * T : (place + 1) * T] = low

    def split_field(ref):
        for b in range(U):
            rows = slice(b * T, (b + 1) * T)
            v_hi[rows], v_lo[rows] = halves(ref[rows])

    def split_panel(k):
        h_hi[k], h_lo[k] = halves(panel_v[k])

    def inner(b, field):
        low_block, high_block = max(b - 1, 0), min(b + 2, U)
        span = slice(low_block * T, high_block * T)
        cols = slice((low_block - b + 1) * T, (high_block - b + 1) * T)
        coupled = dot3((w_hi[b, :, cols], w_lo[b, :, cols]), (v_hi[span], v_lo[span]), NN)
        rows = slice(b * T, (b + 1) * T)
        scale = diag[rows]
        return jnp.concatenate([scale] * (K // T), axis=1) * field[rows] - coupled

    def pack(k):
        panel_index = lax.rem(loop + k, L)
        sums = [jnp.zeros((T, T), jnp.int32)] * (PR // T)
        for e in range(per_panel):
            at = panel_index * per_panel + e
            seen = mask_v[at] != 0
            unit = jnp.left_shift(jnp.int32(1), users_ref[at] * COUNT_BITS)
            for c in range(PR // T):
                weight = jnp.where(items_ref[at] == c, unit, 0)
                sums[c] = sums[c] + jnp.where(seen, weight, 0)
        for c in range(PR // T):
            packed[k, :, c * T : (c + 1) * T] = sums[c]

    def gram(k, blocks):
        rows = slice(blocks[0] * T, (blocks[-1] + 1) * T)
        panel = (h_hi[k], h_lo[k])
        scores = dot3((v_hi[rows], v_lo[rows]), panel, NT)
        counts = []
        for b in blocks:
            word = packed[k]
            if b:
                word = lax.shift_right_logical(word, jnp.int32(COUNT_BITS * b))
            counts.append((word & ((1 << COUNT_BITS) - 1)).astype(F32))
        scores = scores * jnp.concatenate(counts, axis=0)
        return dot3(halves(scores), panel, NN)

    split_field(b_v)
    pairs = [(0, 1)] + [(U - 2, U - 1)] + [(b, b + 1) for b in range(2, U - 2, 2)]

    for b in range(U):
        q_v[b * T : (b + 1) * T] = inner(b, b_v)

    passed = []
    for k in range(1, L):
        direct[k - 1].wait_recv()
        passed += forwards(k)
        for copy in passed[-(g - 1) :] if g > 1 else []:
            copy.start()

    loads[3].wait()
    split_panel(0)
    loads[4].wait()
    for k in range(L):
        pack(k)

    def add_gram(k, blocks, out):
        rows = slice(blocks[0] * T, (blocks[-1] + 1) * T)
        out[rows] = out[rows] + gram(k, blocks)

    for blocks in pairs:
        add_gram(0, blocks, q_v)
    for k in range(1, L):
        for i in range(1, g):
            forward_in(k, i).wait_recv()
        split_panel(k)
    for blocks in pairs[:2]:
        for k in range(1, L):
            add_gram(k, blocks, q_v)

    def edges(ph, out):
        @pl.when(has_before)
        def _():
            product_copies[ph].wait_recv()

        out[:T] = out[:T] - carried[ph]

        @pl.when(has_after)
        def _():
            (first_0, first_1)[ph].wait_recv()

        tile = (w_hi[U - 1, :, 2 * T :], w_lo[U - 1, :, 2 * T :])
        out[tail:] = out[tail:] - dot3(tile, halves(ahead[ph]), NN)

    @pl.when(has_before)
    def _():
        columns_copy.wait_recv()

    entering = jnp.broadcast_to(columns_in[:1], (T, T)).T
    diag[:T] = diag[:T] + entering
    q_v[:T] = q_v[:T] + jnp.concatenate([entering] * (K // T), axis=1) * b_v[:T]
    edges(0, q_v)

    @pl.when(has_before)
    def _():
        first_1.start()

    product[1] = dot3(last_turned, halves(q_v[tail:]), NN)

    @pl.when(has_after)
    def _():
        product_copies[1].start()

    for blocks in pairs[2:]:
        for k in range(1, L):
            add_gram(k, blocks, q_v)

    def store_sums(ph, rows_of_lanes):
        pad = [jnp.zeros((8 - len(rows_of_lanes), 128), F32)]
        mine[ph] = jnp.concatenate(rows_of_lanes + pad, axis=0)

    def near_copy(ph, i, sending):
        t, device = near_device(i)
        slot = me_near if sending else t
        return remote(mine.at[ph], near.at[ph, slot], near_s.at[ph, i], near_r.at[ph, slot], device)

    def far_copy(ph, i, sending):
        t, device = far_device(i)
        slot = me_far if sending else t
        return remote(near_sum.at[ph], far.at[ph, slot], far_s.at[ph, i], far_r.at[ph, slot], device)

    def start_near(ph):
        for i in range(1, G):
            near_copy(ph, i, True).start()

    def near_to_far(ph):
        total = mine[ph]
        for i in range(1, G):
            copy = near_copy(ph, i, False)
            copy.wait_recv()
            total = total + near[ph, lax.rem(me_near + i, G)]
        near_sum[ph] = total
        for i in range(1, Z):
            far_copy(ph, i, True).start()

    def finish_far(ph):
        total = near_sum[ph]
        for i in range(1, Z):
            far_copy(ph, i, False).wait_recv()
            total = total + far[ph, lax.rem(me_far + i, Z)]
        return jnp.sum(total, axis=1, keepdims=True)

    norm = jnp.zeros((1, 128), F32)
    energy = jnp.zeros((1, 128), F32)
    for b in range(U):
        rows = slice(b * T, (b + 1) * T)
        norm = norm + lanes(b_v[rows] * b_v[rows])
        energy = energy + lanes(b_v[rows] * q_v[rows])
    store_sums(0, [norm, energy])
    start_near(0)
    q_copy = pltpu.make_async_copy(q_v, q_out, local_sem.at[5])
    q_copy.start()

    split_field(q_v)
    for b in range(U):
        p_v[b * T : (b + 1) * T] = inner(b, q_v)
    for blocks in pairs:
        add_gram(0, blocks, p_v)
    near_to_far(0)
    for blocks in pairs:
        for k in range(1, L):
            add_gram(k, blocks, p_v)
    edges(1, p_v)
    p_copy = pltpu.make_async_copy(p_v, p_out, local_sem.at[6])
    p_copy.start()

    sums = finish_far(0)
    norm_0, energy_0 = sums[0:1], sums[1:2]
    step_0 = norm_0 / energy_0
    norm = jnp.zeros((1, 128), F32)
    energy = jnp.zeros((1, 128), F32)
    cross = jnp.zeros((1, 128), F32)
    for b in range(U):
        rows = slice(b * T, (b + 1) * T)
        image = q_v[rows]
        residual = b_v[rows] - step_0 * image
        norm = norm + lanes(residual * residual)
        energy = energy + lanes(residual * (image - step_0 * p_v[rows]))
        cross = cross + lanes(residual * image)
    store_sums(1, [norm, energy, cross])
    start_near(1)
    near_to_far(1)
    sums = finish_far(1)
    norm_1, energy_1, cross_1 = sums[0:1], sums[1:2], sums[2:3]
    beta = norm_1 / norm_0
    step_1 = norm_1 / (energy_1 + 2.0 * beta * cross_1 + beta * beta * energy_0)
    first = step_0 + step_1 * (1.0 + beta)
    second = step_0 * step_1
    coef_out[...] = jnp.concatenate([jnp.broadcast_to(first, (4, 128)), jnp.broadcast_to(second, (4, 128))], axis=0)

    for copy in direct + passed:
        copy.wait_send()
    for ph in range(2):
        for i in range(1, G):
            near_copy(ph, i, True).wait_send()
        for i in range(1, Z):
            far_copy(ph, i, True).wait_send()

    @pl.when(has_before)
    def _():
        first_0.wait_send()
        first_1.wait_send()

    @pl.when(has_after)
    def _():
        columns_copy.wait_send()
        for copy in product_copies:
            copy.wait_send()

    q_copy.wait()
    p_copy.wait()


def body(panels, right_side, block_users, block_items, masks, self_tiles, next_tiles):
    R, L = lax.axis_size("row"), lax.axis_size("loop")
    g = 4 if R % 4 == 0 else R
    Z, G = R // g, 4 * L if R % 4 == 0 else R * L
    T = masks.shape[1]
    PR, K = panels.shape
    rows = right_side.shape[0]
    U = rows // T
    entries = masks.shape[0]
    per_panel = entries // L
    assert per_panel < 1 << COUNT_BITS and U * COUNT_BITS <= 32
    sizes = (R, L, g, T, U, K, PR, per_panel)
    hbm = pl.BlockSpec(memory_space=pl.ANY)
    smem = pl.BlockSpec(memory_space=pltpu.SMEM)
    vmem = pl.BlockSpec(memory_space=pltpu.VMEM)
    field = jax.ShapeDtypeStruct((rows, K), F32)
    dma = pltpu.SemaphoreType.DMA
    q, p, coef = pl.pallas_call(
        functools.partial(kernel, sizes),
        out_shape=(field, field, jax.ShapeDtypeStruct((8, 128), F32)),
        in_specs=[smem, smem] + [hbm] * 5,
        out_specs=(hbm, hbm, vmem),
        scratch_shapes=[
            pltpu.VMEM((rows, K), F32),
            pltpu.VMEM((rows, K), F32),
            pltpu.VMEM((rows, K), F32),
            pltpu.VMEM((rows, K), BF16),
            pltpu.VMEM((rows, K), BF16),
            pltpu.VMEM((L, PR, K), F32),
            pltpu.VMEM((L, PR, K), BF16),
            pltpu.VMEM((L, PR, K), BF16),
            pltpu.VMEM((entries, T, T), jnp.int32),
            pltpu.VMEM((L, T, PR), jnp.int32),
            pltpu.VMEM((rows, T), F32),
            pltpu.VMEM((rows, T), F32),
            pltpu.VMEM((U, T, 3 * T), BF16),
            pltpu.VMEM((U, T, 3 * T), BF16),
            pltpu.VMEM((rows, T), F32),
            pltpu.VMEM((2, T, K), F32),
            pltpu.VMEM((2, T, K), F32),
            pltpu.VMEM((2, T, K), F32),
            pltpu.VMEM((8, T), F32),
            pltpu.VMEM((8, T), F32),
            pltpu.VMEM((2, 8, 128), F32),
            pltpu.VMEM((2, G, 8, 128), F32),
            pltpu.VMEM((2, 8, 128), F32),
            pltpu.VMEM((2, Z, 8, 128), F32),
            dma((7,)),
            dma((L,)),
            dma((L,)),
            dma((L, g)),
            dma((L, g)),
            dma((2, 3)),
            dma((2, 3)),
            dma((2, G)),
            dma((2, G)),
            dma((2, Z)),
            dma((2, Z)),
        ],
        compiler_params=pltpu.CompilerParams(
            collective_id=0, has_side_effects=True, vmem_limit_bytes=32 * 1024 * 1024
        ),
        cost_estimate=pl.CostEstimate(flops=8 * rows * K * PR * L, bytes_accessed=8 * rows * K * 4, transcendentals=0),
    )(block_users, block_items, panels, right_side, masks, self_tiles, next_tiles)
    first, second = coef[0, 0], coef[4, 0]
    solution_field = first * right_side - second * q
    residual = right_side - first * q + second * p
    return solution_field, residual


def solution(mesh):
    placed = (
        P("loop", None),
        P(("row", "loop"), None),
        P(("row", "loop")),
        P(("row", "loop")),
        P(("row", "loop"), None, None),
        P(("row", "loop"), None),
        P(("row", "loop"), None),
    )
    return jax.shard_map(
        body,
        mesh=mesh,
        in_specs=placed,
        out_specs=(P(("row", "loop"), None), P(("row", "loop"), None)),
        check_vma=False,
    )
```

```python
import functools

import jax
import jax.numpy as jnp
from jax import lax
from jax.experimental import pallas as pl
from jax.experimental.pallas import tpu as pltpu
from jax.sharding import PartitionSpec as P

ridge_weight = 0.5
MESH = pl.DeviceIdType.MESH
F32 = jnp.float32
BF16 = jnp.bfloat16
COUNT_BITS = 4
NN = (((1,), (0,)), ((), ()))
NT = (((1,), (1,)), ((), ()))
TN = (((0,), (0,)), ((), ()))


def halves(x):
    high = x.astype(BF16)
    return high, (x - high.astype(F32)).astype(BF16)


def dot3(a, b, dims):
    dot = functools.partial(lax.dot_general, dimension_numbers=dims, preferred_element_type=F32)
    return dot(a[0], b[0]) + (dot(a[1], b[0]) + dot(a[0], b[1]))


def lanes(x):
    rows, width = x.shape
    x = sum(x[:, c : c + 128] for c in range(0, width, 128))
    return jnp.sum(x, axis=0, keepdims=True)


def kernel(
    sizes,
    users_ref,
    items_ref,
    panel_ref,
    right_ref,
    mask_ref,
    self_ref,
    next_ref,
    q_out,
    p_out,
    coef_out,
    b_v,
    q_v,
    p_v,
    v_hi,
    v_lo,
    panel_v,
    h_hi,
    h_lo,
    mask_v,
    packed,
    self_v,
    next_v,
    w_hi,
    w_lo,
    diag,
    ahead,
    behind,
    edge_out,
    next_in,
    mine,
    near,
    near_sum,
    far,
    local_sem,
    panel_s,
    panel_r,
    share_s,
    share_r,
    halo_s,
    halo_r,
    near_s,
    near_r,
    far_s,
    far_r,
):
    R, L, g, gr, T, U, K, PR, per_panel = sizes
    Z = R // gr
    G = gr * L
    row, loop = lax.axis_index("row"), lax.axis_index("loop")
    n = R * L
    d = row * L + loop
    me_near = lax.rem(row, gr) * L + loop
    me_far = row // gr
    quarter = lax.rem(row, g)
    base = row // g * g
    after, before = lax.rem(d + 1, n), lax.rem(d + n - 1, n)
    after = (after // L, lax.rem(after, L))
    before = (before // L, lax.rem(before, L))
    has_after, has_before = d < n - 1, d > 0
    tail = (U - 1) * T

    loads = [
        pltpu.make_async_copy(src, dst, local_sem.at[i])
        for i, (src, dst) in enumerate(
            [
                (next_ref, next_v),
                (right_ref, b_v),
                (self_ref, self_v),
                (panel_ref, panel_v.at[0]),
                (mask_ref, mask_v),
            ]
        )
    ]
    for load in loads:
        load.start()

    def near_device(i):
        t = lax.rem(me_near + i, G)
        return t, (me_far * gr + t // L, lax.rem(t, L))

    def far_device(i):
        t = lax.rem(me_far + i, Z)
        return t, (t * gr + lax.rem(row, gr), loop)

    barrier = pltpu.get_barrier_semaphore()
    greeted = [near_device(i)[1] for i in range(1, G)] + [far_device(i)[1] for i in range(1, Z)]
    greeted += [after, before]
    for device in greeted:
        pl.semaphore_signal(barrier, inc=1, device_id=device, device_id_type=MESH)
    pl.semaphore_wait(barrier, len(greeted))

    def remote(src, dst, send, recv, device):
        return pltpu.make_async_remote_copy(
            src_ref=src, dst_ref=dst, send_sem=send, recv_sem=recv, device_id=device, device_id_type=MESH
        )

    part = PR // g

    def share(k, which):
        return panel_v.at[k, pl.ds(pl.multiple_of(which * part, part), part)]

    own_share = panel_ref.at[pl.ds(pl.multiple_of(quarter * part, part), part)]
    direct = [
        remote(own_share, share(k, quarter), panel_s.at[k], panel_r.at[k], (row, lax.rem(loop + L - k, L)))
        for k in range(1, L)
    ]
    for copy in direct:
        copy.start()

    def forwards(k):
        copies = []
        for i in range(1, g):
            t = lax.rem(quarter + i, g)
            copies.append(
                remote(share(k, quarter), share(k, quarter), share_s.at[k, i], share_r.at[k, quarter], (base + t, loop))
            )
        return copies

    def forward_in(k, i):
        t = lax.rem(quarter + i, g)
        return remote(share(k, t), share(k, t), share_s.at[k, i], share_r.at[k, t], (base + t, loop))

    to_before = [
        remote(src, ahead.at[ph], halo_s.at[ph, 0], halo_r.at[ph, 0], before)
        for ph, src in enumerate([right_ref.at[pl.ds(0, T)], edge_out.at[0]])
    ]
    to_after = [
        remote(src, behind.at[ph], halo_s.at[ph, 1], halo_r.at[ph, 1], after)
        for ph, src in enumerate([right_ref.at[pl.ds(tail, T)], edge_out.at[1]])
    ]
    tile_copy = remote(next_ref.at[pl.ds(tail, T)], next_in, halo_s.at[0, 2], halo_r.at[0, 2], after)

    @pl.when(has_before)
    def _():
        to_before[0].start()

    @pl.when(jnp.logical_not(has_before))
    def _():
        behind[...] = jnp.zeros_like(behind)
        next_in[...] = jnp.zeros_like(next_in)

    @pl.when(has_after)
    def _():
        tile_copy.start()
        to_after[0].start()

    @pl.when(jnp.logical_not(has_after))
    def _():
        ahead[...] = jnp.zeros_like(ahead)

    loads[0].wait()
    loads[1].wait()

    loads[2].wait()
    degrees = []
    onward_columns = None
    for b in range(U):
        rows = slice(b * T, (b + 1) * T)
        own = self_v[rows]
        sym = 0.5 * (own + own.T)
        onward = next_v[rows]
        turned = onward.T
        degree = jnp.sum(sym, axis=1, keepdims=True) + jnp.sum(onward, axis=1, keepdims=True)
        if onward_columns is not None:
            degree = degree + onward_columns
        onward_columns = jnp.sum(turned, axis=1, keepdims=True)
        diag[rows] = jnp.broadcast_to(degree + ridge_weight, (T, T))
        for place, tile, target in ((1, sym, b), (2, onward, b), (0, turned, b + 1)):
            if target < U:
                high, low = halves(tile)
                w_hi[target, :, place * T : (place + 1) * T] = high
                w_lo[target, :, place * T : (place + 1) * T] = low

    def split_field(ref):
        for b in range(U):
            rows = slice(b * T, (b + 1) * T)
            v_hi[rows], v_lo[rows] = halves(ref[rows])

    def split_panel(k):
        h_hi[k], h_lo[k] = halves(panel_v[k])

    def inner(b, field):
        low_block, high_block = max(b - 1, 0), min(b + 2, U)
        span = slice(low_block * T, high_block * T)
        cols = slice((low_block - b + 1) * T, (high_block - b + 1) * T)
        coupled = dot3((w_hi[b, :, cols], w_lo[b, :, cols]), (v_hi[span], v_lo[span]), NN)
        rows = slice(b * T, (b + 1) * T)
        scale = diag[rows]
        return jnp.concatenate([scale] * (K // T), axis=1) * field[rows] - coupled

    def pack(k):
        panel_index = lax.rem(loop + k, L)
        sums = [jnp.zeros((T, T), jnp.int32)] * (PR // T)
        for e in range(per_panel):
            at = panel_index * per_panel + e
            seen = mask_v[at] != 0
            unit = jnp.left_shift(jnp.int32(1), users_ref[at] * COUNT_BITS)
            for c in range(PR // T):
                weight = jnp.where(items_ref[at] == c, unit, 0)
                sums[c] = sums[c] + jnp.where(seen, weight, 0)
        for c in range(PR // T):
            packed[k, :, c * T : (c + 1) * T] = sums[c]

    def gram(k, blocks):
        rows = slice(blocks[0] * T, (blocks[-1] + 1) * T)
        panel = (h_hi[k], h_lo[k])
        scores = dot3((v_hi[rows], v_lo[rows]), panel, NT)
        counts = []
        for b in blocks:
            word = packed[k]
            if b:
                word = lax.shift_right_logical(word, jnp.int32(COUNT_BITS * b))
            counts.append((word & ((1 << COUNT_BITS) - 1)).astype(F32))
        scores = scores * jnp.concatenate(counts, axis=0)
        return dot3(halves(scores), panel, NN)

    split_field(b_v)
    passed = []
    for k in range(1, L):
        direct[k - 1].wait_recv()
        sent = forwards(k)
        for copy in sent:
            copy.start()
        passed += sent

    pairs = [(0, 1)] + [(U - 2, U - 1)] + [(b, b + 1) for b in range(2, U - 2, 2)]

    for b in range(U):
        q_v[b * T : (b + 1) * T] = inner(b, b_v)

    loads[3].wait()
    split_panel(0)
    loads[4].wait()
    for k in range(L):
        pack(k)

    def add_gram(k, blocks, out):
        rows = slice(blocks[0] * T, (blocks[-1] + 1) * T)
        out[rows] = out[rows] + gram(k, blocks)

    for blocks in pairs:
        add_gram(0, blocks, q_v)
    for k in range(1, L):
        for i in range(1, g):
            forward_in(k, i).wait_recv()
        split_panel(k)
    for blocks in pairs[:2]:
        for k in range(1, L):
            add_gram(k, blocks, q_v)

    edge_out[0] = q_v[:T]
    edge_out[1] = q_v[tail:]

    @pl.when(has_before)
    def _():
        to_before[1].start()

    @pl.when(has_after)
    def _():
        to_after[1].start()

    for blocks in pairs[2:]:
        for k in range(1, L):
            add_gram(k, blocks, q_v)

    def store_sums(ph, rows_of_lanes):
        pad = [jnp.zeros((8 - len(rows_of_lanes), 128), F32)]
        mine[ph] = jnp.concatenate(rows_of_lanes + pad, axis=0)

    def near_copy(ph, i, sending):
        t, device = near_device(i)
        slot = me_near if sending else t
        return remote(mine.at[ph], near.at[ph, slot], near_s.at[ph, i], near_r.at[ph, slot], device)

    def far_copy(ph, i, sending):
        t, device = far_device(i)
        slot = me_far if sending else t
        return remote(near_sum.at[ph], far.at[ph, slot], far_s.at[ph, i], far_r.at[ph, slot], device)

    def start_near(ph):
        for i in range(1, G):
            near_copy(ph, i, True).start()

    def near_to_far(ph):
        total = mine[ph]
        for i in range(1, G):
            copy = near_copy(ph, i, False)
            copy.wait_recv()
            total = total + near[ph, lax.rem(me_near + i, G)]
        near_sum[ph] = total
        for i in range(1, Z):
            far_copy(ph, i, True).start()

    def finish_far(ph):
        total = near_sum[ph]
        for i in range(1, Z):
            far_copy(ph, i, False).wait_recv()
            total = total + far[ph, lax.rem(me_far + i, Z)]
        return jnp.sum(total, axis=1, keepdims=True)

    @pl.when(has_before)
    def _():
        tile_copy.wait_recv()
        to_after[0].wait_recv()

    @pl.when(has_after)
    def _():
        to_before[0].wait_recv()

    def wide(column):
        return jnp.concatenate([column] * (K // T), axis=1)

    def spread_columns(tile):
        return jnp.broadcast_to(jnp.sum(tile.T, axis=1, keepdims=True), (T, T))

    entering_tile = next_in[...]
    entering = halves(entering_tile)
    turned_in = halves(entering_tile.T)
    last_next = next_v[tail:]
    leaving = halves(last_next)
    turned_out = halves(last_next.T)
    columns = spread_columns(entering_tile)
    diag[:T] = diag[:T] + columns
    q_v[:T] = q_v[:T] + wide(columns) * b_v[:T] - dot3(turned_in, halves(behind[0]), NN)
    q_v[tail:] = q_v[tail:] - dot3(leaving, halves(ahead[0]), NN)
    behind_more = dot3(entering, (v_hi[:T], v_lo[:T]), NN)
    ahead_more = wide(spread_columns(last_next)) * ahead[0] - dot3(turned_out, (v_hi[tail:], v_lo[tail:]), NN)
    q_copy = pltpu.make_async_copy(q_v, q_out, local_sem.at[5])
    q_copy.start()

    split_field(q_v)
    for b in range(U):
        p_v[b * T : (b + 1) * T] = inner(b, q_v)
    for k in range(L):
        for blocks in pairs:
            add_gram(k, blocks, p_v)

    totals = [jnp.zeros((1, 128), F32)] * 4
    edge_blocks = (0, U - 1)

    def add_sum(at, left, right, b):
        rows = slice(b * T, (b + 1) * T)
        totals[at] = totals[at] + lanes(left[rows] * right[rows])

    for b in range(U):
        add_sum(0, b_v, b_v, b)
        add_sum(1, b_v, q_v, b)
        add_sum(2, q_v, q_v, b)
        if b not in edge_blocks:
            add_sum(3, q_v, p_v, b)

    @pl.when(has_before)
    def _():
        to_after[1].wait_recv()

    @pl.when(has_after)
    def _():
        to_before[1].wait_recv()

    coupled_after = jnp.where(has_after, F32(1), F32(0))
    p_v[:T] = p_v[:T] - dot3(turned_in, halves(behind[1] - behind_more), NN)
    p_v[tail:] = p_v[tail:] - dot3(leaving, halves(coupled_after * (ahead[1] + ahead_more)), NN)
    for b in edge_blocks:
        add_sum(3, q_v, p_v, b)
    p_copy = pltpu.make_async_copy(p_v, p_out, local_sem.at[6])
    store_sums(0, totals)
    start_near(0)
    p_copy.start()
    near_to_far(0)
    sums = finish_far(0)
    norm_0, energy_0, square, energy_q = sums[0:1], sums[1:2], sums[2:3], sums[3:4]
    step_0 = norm_0 / energy_0
    norm_1 = norm_0 - 2.0 * step_0 * energy_0 + step_0 * step_0 * square
    beta = norm_1 / norm_0
    more = 1.0 + beta
    energy_1 = more * (more * energy_0 - 2.0 * step_0 * square) + step_0 * step_0 * energy_q
    step_1 = norm_1 / energy_1
    first = step_0 + step_1 * more
    second = step_0 * step_1
    coef_out[...] = jnp.concatenate([jnp.broadcast_to(first, (4, 128)), jnp.broadcast_to(second, (4, 128))], axis=0)

    for copy in direct + passed:
        copy.wait_send()
    for ph in (0,):
        for i in range(1, G):
            near_copy(ph, i, True).wait_send()
        for i in range(1, Z):
            far_copy(ph, i, True).wait_send()

    @pl.when(has_before)
    def _():
        for copy in to_before:
            copy.wait_send()

    @pl.when(has_after)
    def _():
        tile_copy.wait_send()
        for copy in to_after:
            copy.wait_send()

    q_copy.wait()
    p_copy.wait()


def finish(coef_ref, right_ref, q_ref, p_ref, solution_ref, residual_ref):
    first, second = coef_ref[0:1, 0:1], coef_ref[4:5, 0:1]
    right, q = right_ref[...], q_ref[...]
    solution_ref[...] = first * right - second * q
    residual_ref[...] = right - first * q + second * p_ref[...]


def body(panels, right_side, block_users, block_items, masks, self_tiles, next_tiles):
    R, L = lax.axis_size("row"), lax.axis_size("loop")
    g = 4 if R % 4 == 0 else R
    gr = g
    Z, G = R // gr, gr * L
    T = masks.shape[1]
    PR, K = panels.shape
    rows = right_side.shape[0]
    U = rows // T
    entries = masks.shape[0]
    per_panel = entries // L
    assert per_panel < 1 << COUNT_BITS and U * COUNT_BITS <= 32
    sizes = (R, L, g, gr, T, U, K, PR, per_panel)
    hbm = pl.BlockSpec(memory_space=pl.ANY)
    smem = pl.BlockSpec(memory_space=pltpu.SMEM)
    vmem = pl.BlockSpec(memory_space=pltpu.VMEM)
    field = jax.ShapeDtypeStruct((rows, K), F32)
    dma = pltpu.SemaphoreType.DMA
    q, p, coef = pl.pallas_call(
        functools.partial(kernel, sizes),
        out_shape=(field, field, jax.ShapeDtypeStruct((8, 128), F32)),
        in_specs=[smem, smem] + [hbm] * 5,
        out_specs=(hbm, hbm, vmem),
        scratch_shapes=[
            pltpu.VMEM((rows, K), F32),
            pltpu.VMEM((rows, K), F32),
            pltpu.VMEM((rows, K), F32),
            pltpu.VMEM((rows, K), BF16),
            pltpu.VMEM((rows, K), BF16),
            pltpu.VMEM((L, PR, K), F32),
            pltpu.VMEM((L, PR, K), BF16),
            pltpu.VMEM((L, PR, K), BF16),
            pltpu.VMEM((entries, T, T), jnp.int32),
            pltpu.VMEM((L, T, PR), jnp.int32),
            pltpu.VMEM((rows, T), F32),
            pltpu.VMEM((rows, T), F32),
            pltpu.VMEM((U, T, 3 * T), BF16),
            pltpu.VMEM((U, T, 3 * T), BF16),
            pltpu.VMEM((rows, T), F32),
            pltpu.VMEM((2, T, K), F32),
            pltpu.VMEM((2, T, K), F32),
            pltpu.VMEM((2, T, K), F32),
            pltpu.VMEM((T, T), F32),
            pltpu.VMEM((1, 8, 128), F32),
            pltpu.VMEM((1, G, 8, 128), F32),
            pltpu.VMEM((1, 8, 128), F32),
            pltpu.VMEM((1, Z, 8, 128), F32),
            dma((7,)),
            dma((L,)),
            dma((L,)),
            dma((L, g)),
            dma((L, g)),
            dma((2, 3)),
            dma((2, 3)),
            dma((1, G)),
            dma((1, G)),
            dma((1, Z)),
            dma((1, Z)),
        ],
        compiler_params=pltpu.CompilerParams(
            collective_id=0, has_side_effects=True, vmem_limit_bytes=60 * 1024 * 1024
        ),
        cost_estimate=pl.CostEstimate(flops=8 * rows * K * PR * L, bytes_accessed=8 * rows * K * 4, transcendentals=0),
    )(block_users, block_items, panels, right_side, masks, self_tiles, next_tiles)
    steps = 4
    block = pl.BlockSpec((rows // steps, K), lambda i: (i, 0))
    return pl.pallas_call(
        finish,
        grid=(steps,),
        out_shape=(field, field),
        in_specs=[pl.BlockSpec((8, 128), lambda i: (0, 0)), block, block, block],
        out_specs=(block, block),
    )(coef, right_side, q, p)


def solution(mesh):
    placed = (
        P("loop", None),
        P(("row", "loop"), None),
        P(("row", "loop")),
        P(("row", "loop")),
        P(("row", "loop"), None, None),
        P(("row", "loop"), None),
        P(("row", "loop"), None),
    )
    return jax.shard_map(
        body,
        mesh=mesh,
        in_specs=placed,
        out_specs=(P(("row", "loop"), None), P(("row", "loop"), None)),
        check_vma=False,
    )
```

```python
import functools

import jax
import jax.numpy as jnp
from jax import lax
from jax.experimental import pallas as pl
from jax.experimental.pallas import tpu as pltpu
from jax.sharding import PartitionSpec as P

ridge_weight = 0.5
MESH = pl.DeviceIdType.MESH
F32 = jnp.float32
BF16 = jnp.bfloat16
COUNT_BITS = 4
NN = (((1,), (0,)), ((), ()))
NT = (((1,), (1,)), ((), ()))
TN = (((0,), (0,)), ((), ()))


def halves(x):
    high = x.astype(BF16)
    return high, (x - high.astype(F32)).astype(BF16)


def dot3(a, b, dims):
    dot = functools.partial(lax.dot_general, dimension_numbers=dims, preferred_element_type=F32)
    return dot(a[0], b[0]) + (dot(a[1], b[0]) + dot(a[0], b[1]))


def lanes(x):
    rows, width = x.shape
    x = sum(x[:, c : c + 128] for c in range(0, width, 128))
    return jnp.sum(x, axis=0, keepdims=True)


def kernel(
    sizes,
    users_ref,
    items_ref,
    panel_ref,
    right_ref,
    mask_ref,
    self_ref,
    next_ref,
    q_out,
    p_out,
    coef_out,
    b_v,
    q_v,
    p_v,
    v_hi,
    v_lo,
    panel_v,
    h_hi,
    h_lo,
    mask_v,
    packed,
    self_v,
    next_v,
    w_hi,
    w_lo,
    diag,
    ahead,
    behind,
    edge_out,
    next_in,
    mine,
    near,
    near_sum,
    far,
    local_sem,
    panel_s,
    panel_r,
    share_s,
    share_r,
    halo_s,
    halo_r,
    near_s,
    near_r,
    far_s,
    far_r,
):
    R, L, g, gr, T, U, K, PR, per_panel = sizes
    Z = R // gr
    G = gr * L
    row, loop = lax.axis_index("row"), lax.axis_index("loop")
    n = R * L
    d = row * L + loop
    me_near = lax.rem(row, gr) * L + loop
    me_far = row // gr
    quarter = lax.rem(row, g)
    base = row // g * g
    after, before = lax.rem(d + 1, n), lax.rem(d + n - 1, n)
    after = (after // L, lax.rem(after, L))
    before = (before // L, lax.rem(before, L))
    has_after, has_before = d < n - 1, d > 0
    tail = (U - 1) * T

    loads = [
        pltpu.make_async_copy(src, dst, local_sem.at[i])
        for i, (src, dst) in enumerate(
            [
                (next_ref, next_v),
                (right_ref, b_v),
                (self_ref, self_v),
                (panel_ref, panel_v.at[0]),
                (mask_ref, mask_v),
            ]
        )
    ]
    for load in loads:
        load.start()

    def near_device(i):
        t = lax.rem(me_near + i, G)
        return t, (me_far * gr + t // L, lax.rem(t, L))

    def far_device(i):
        t = lax.rem(me_far + i, Z)
        return t, (t * gr + lax.rem(row, gr), loop)

    barrier = pltpu.get_barrier_semaphore()
    greeted = [near_device(i)[1] for i in range(1, G)] + [far_device(i)[1] for i in range(1, Z)]
    greeted += [after, before]
    for device in greeted:
        pl.semaphore_signal(barrier, inc=1, device_id=device, device_id_type=MESH)
    pl.semaphore_wait(barrier, len(greeted))

    def remote(src, dst, send, recv, device):
        return pltpu.make_async_remote_copy(
            src_ref=src, dst_ref=dst, send_sem=send, recv_sem=recv, device_id=device, device_id_type=MESH
        )

    part = PR // g

    def share(k, which):
        return panel_v.at[k, pl.ds(pl.multiple_of(which * part, part), part)]

    own_share = panel_ref.at[pl.ds(pl.multiple_of(quarter * part, part), part)]
    direct = [
        remote(own_share, share(k, quarter), panel_s.at[k], panel_r.at[k], (row, lax.rem(loop + L - k, L)))
        for k in range(1, L)
    ]
    for copy in direct:
        copy.start()

    def forwards(k):
        copies = []
        for i in range(1, g):
            t = lax.rem(quarter + i, g)
            copies.append(
                remote(share(k, quarter), share(k, quarter), share_s.at[k, i], share_r.at[k, quarter], (base + t, loop))
            )
        return copies

    def forward_in(k, i):
        t = lax.rem(quarter + i, g)
        return remote(share(k, t), share(k, t), share_s.at[k, i], share_r.at[k, t], (base + t, loop))

    to_before = [
        remote(src, ahead.at[ph], halo_s.at[ph, 0], halo_r.at[ph, 0], before)
        for ph, src in enumerate([right_ref.at[pl.ds(0, T)], edge_out.at[0]])
    ]
    to_after = [
        remote(src, behind.at[ph], halo_s.at[ph, 1], halo_r.at[ph, 1], after)
        for ph, src in enumerate([right_ref.at[pl.ds(tail, T)], edge_out.at[1]])
    ]
    tile_copy = remote(next_ref.at[pl.ds(tail, T)], next_in, halo_s.at[0, 2], halo_r.at[0, 2], after)

    @pl.when(has_before)
    def _():
        to_before[0].start()

    @pl.when(jnp.logical_not(has_before))
    def _():
        behind[...] = jnp.zeros_like(behind)
        next_in[...] = jnp.zeros_like(next_in)

    @pl.when(has_after)
    def _():
        tile_copy.start()
        to_after[0].start()

    @pl.when(jnp.logical_not(has_after))
    def _():
        ahead[...] = jnp.zeros_like(ahead)

    loads[0].wait()
    loads[1].wait()

    loads[2].wait()
    degrees = []
    onward_columns = None
    for b in range(U):
        rows = slice(b * T, (b + 1) * T)
        own = self_v[rows]
        sym = 0.5 * (own + own.T)
        onward = next_v[rows]
        turned = onward.T
        degree = jnp.sum(sym, axis=1, keepdims=True) + jnp.sum(onward, axis=1, keepdims=True)
        if onward_columns is not None:
            degree = degree + onward_columns
        onward_columns = jnp.sum(turned, axis=1, keepdims=True)
        diag[rows] = jnp.broadcast_to(degree + ridge_weight, (T, T))
        for place, tile, target in ((1, sym, b), (2, onward, b), (0, turned, b + 1)):
            if target < U:
                high, low = halves(tile)
                w_hi[target, :, place * T : (place + 1) * T] = high
                w_lo[target, :, place * T : (place + 1) * T] = low

    def split_field(ref):
        for b in range(U):
            rows = slice(b * T, (b + 1) * T)
            v_hi[rows], v_lo[rows] = halves(ref[rows])

    def split_panel(k):
        h_hi[k], h_lo[k] = halves(panel_v[k])

    def inner(b, field):
        low_block, high_block = max(b - 1, 0), min(b + 2, U)
        span = slice(low_block * T, high_block * T)
        cols = slice((low_block - b + 1) * T, (high_block - b + 1) * T)
        coupled = dot3((w_hi[b, :, cols], w_lo[b, :, cols]), (v_hi[span], v_lo[span]), NN)
        rows = slice(b * T, (b + 1) * T)
        scale = diag[rows]
        return jnp.concatenate([scale] * (K // T), axis=1) * field[rows] - coupled

    def pack(k):
        panel_index = lax.rem(loop + k, L)
        sums = [jnp.zeros((T, T), jnp.int32)] * (PR // T)
        for e in range(per_panel):
            at = panel_index * per_panel + e
            seen = mask_v[at] != 0
            unit = jnp.left_shift(jnp.int32(1), users_ref[at] * COUNT_BITS)
            for c in range(PR // T):
                weight = jnp.where(items_ref[at] == c, unit, 0)
                sums[c] = sums[c] + jnp.where(seen, weight, 0)
        for c in range(PR // T):
            packed[k, :, c * T : (c + 1) * T] = sums[c]

    def gram(k, blocks):
        rows = slice(blocks[0] * T, (blocks[-1] + 1) * T)
        panel = (h_hi[k], h_lo[k])
        scores = dot3((v_hi[rows], v_lo[rows]), panel, NT)
        counts = []
        for b in blocks:
            word = packed[k]
            if b:
                word = lax.shift_right_logical(word, jnp.int32(COUNT_BITS * b))
            counts.append((word & ((1 << COUNT_BITS) - 1)).astype(F32))
        scores = scores * jnp.concatenate(counts, axis=0)
        return dot3(halves(scores), panel, NN)

    split_field(b_v)
    passed = []
    for k in range(1, L):
        direct[k - 1].wait_recv()
        sent = forwards(k)
        for copy in sent:
            copy.start()
        passed += sent

    pairs = [(0, 1)] + [(U - 2, U - 1)] + [(b, b + 1) for b in range(2, U - 2, 2)]

    for b in range(U):
        q_v[b * T : (b + 1) * T] = inner(b, b_v)

    loads[3].wait()
    split_panel(0)
    loads[4].wait()
    for k in range(L):
        pack(k)

    def add_gram(k, blocks, out):
        rows = slice(blocks[0] * T, (blocks[-1] + 1) * T)
        out[rows] = out[rows] + gram(k, blocks)

    for blocks in pairs:
        add_gram(0, blocks, q_v)
    for k in range(1, L):
        for i in range(1, g):
            forward_in(k, i).wait_recv()
        split_panel(k)
    for blocks in pairs[:2]:
        for k in range(1, L):
            add_gram(k, blocks, q_v)

    edge_out[0] = q_v[:T]
    edge_out[1] = q_v[tail:]

    @pl.when(has_before)
    def _():
        to_before[1].start()

    @pl.when(has_after)
    def _():
        to_after[1].start()

    for blocks in pairs[2:]:
        for k in range(1, L):
            add_gram(k, blocks, q_v)

    def store_sums(ph, rows_of_lanes):
        pad = [jnp.zeros((8 - len(rows_of_lanes), 128), F32)]
        mine[ph] = jnp.concatenate(rows_of_lanes + pad, axis=0)

    def near_copy(ph, i, sending):
        t, device = near_device(i)
        slot = me_near if sending else t
        return remote(mine.at[ph], near.at[ph, slot], near_s.at[ph, i], near_r.at[ph, slot], device)

    def far_copy(ph, i, sending):
        t, device = far_device(i)
        slot = me_far if sending else t
        return remote(near_sum.at[ph], far.at[ph, slot], far_s.at[ph, i], far_r.at[ph, slot], device)

    def start_near(ph):
        for i in range(1, G):
            near_copy(ph, i, True).start()

    def near_to_far(ph):
        total = mine[ph]
        for i in range(1, G):
            copy = near_copy(ph, i, False)
            copy.wait_recv()
            total = total + near[ph, lax.rem(me_near + i, G)]
        near_sum[ph] = total
        for i in range(1, Z):
            far_copy(ph, i, True).start()

    def finish_far(ph):
        total = near_sum[ph]
        for i in range(1, Z):
            far_copy(ph, i, False).wait_recv()
            total = total + far[ph, lax.rem(me_far + i, Z)]
        return jnp.sum(total, axis=1, keepdims=True)

    @pl.when(has_before)
    def _():
        tile_copy.wait_recv()
        to_after[0].wait_recv()

    @pl.when(has_after)
    def _():
        to_before[0].wait_recv()

    def wide(column):
        return jnp.concatenate([column] * (K // T), axis=1)

    def spread_columns(tile):
        return jnp.broadcast_to(jnp.sum(tile.T, axis=1, keepdims=True), (T, T))

    entering_tile = next_in[...]
    entering = halves(entering_tile)
    turned_in = halves(entering_tile.T)
    last_next = next_v[tail:]
    leaving = halves(last_next)
    turned_out = halves(last_next.T)
    columns = spread_columns(entering_tile)
    diag[:T] = diag[:T] + columns
    q_v[:T] = q_v[:T] + wide(columns) * b_v[:T] - dot3(turned_in, halves(behind[0]), NN)
    q_v[tail:] = q_v[tail:] - dot3(leaving, halves(ahead[0]), NN)
    behind_more = dot3(entering, (v_hi[:T], v_lo[:T]), NN)
    ahead_more = wide(spread_columns(last_next)) * ahead[0] - dot3(turned_out, (v_hi[tail:], v_lo[tail:]), NN)
    q_copy = pltpu.make_async_copy(q_v, q_out, local_sem.at[5])
    q_copy.start()

    split_field(q_v)
    for b in range(U):
        p_v[b * T : (b + 1) * T] = inner(b, q_v)
    for k in range(L):
        for blocks in pairs:
            add_gram(k, blocks, p_v)

    totals = [jnp.zeros((1, 128), F32)] * 4
    edge_blocks = (0, U - 1)

    def add_sum(at, left, right, b):
        rows = slice(b * T, (b + 1) * T)
        totals[at] = totals[at] + lanes(left[rows] * right[rows])

    for b in range(U):
        add_sum(0, b_v, b_v, b)
        add_sum(1, b_v, q_v, b)
        add_sum(2, q_v, q_v, b)
        if b not in edge_blocks:
            add_sum(3, q_v, p_v, b)

    @pl.when(has_before)
    def _():
        to_after[1].wait_recv()

    @pl.when(has_after)
    def _():
        to_before[1].wait_recv()

    coupled_after = jnp.where(has_after, F32(1), F32(0))
    p_v[:T] = p_v[:T] - dot3(turned_in, halves(behind[1] - behind_more), NN)
    p_v[tail:] = p_v[tail:] - dot3(leaving, halves(coupled_after * (ahead[1] + ahead_more)), NN)
    for b in edge_blocks:
        add_sum(3, q_v, p_v, b)
    p_copy = pltpu.make_async_copy(p_v, p_out, local_sem.at[6])
    store_sums(0, totals)
    start_near(0)
    p_copy.start()
    near_to_far(0)
    sums = finish_far(0)
    norm_0, energy_0, square, energy_q = sums[0:1], sums[1:2], sums[2:3], sums[3:4]
    step_0 = norm_0 / energy_0
    norm_1 = norm_0 - 2.0 * step_0 * energy_0 + step_0 * step_0 * square
    beta = norm_1 / norm_0
    more = 1.0 + beta
    energy_1 = more * (more * energy_0 - 2.0 * step_0 * square) + step_0 * step_0 * energy_q
    step_1 = norm_1 / energy_1
    first = step_0 + step_1 * more
    second = step_0 * step_1
    coef_out[...] = jnp.concatenate([jnp.broadcast_to(first, (4, 128)), jnp.broadcast_to(second, (4, 128))], axis=0)

    for copy in direct + passed:
        copy.wait_send()
    for ph in (0,):
        for i in range(1, G):
            near_copy(ph, i, True).wait_send()
        for i in range(1, Z):
            far_copy(ph, i, True).wait_send()

    @pl.when(has_before)
    def _():
        for copy in to_before:
            copy.wait_send()

    @pl.when(has_after)
    def _():
        tile_copy.wait_send()
        for copy in to_after:
            copy.wait_send()

    q_copy.wait()
    p_copy.wait()


def finish(coef_ref, right_ref, q_ref, p_ref, solution_ref, residual_ref):
    first, second = coef_ref[0:1, 0:1], coef_ref[4:5, 0:1]
    right, q = right_ref[...], q_ref[...]
    solution_ref[...] = first * right - second * q
    residual_ref[...] = right - first * q + second * p_ref[...]


def body(panels, right_side, block_users, block_items, masks, self_tiles, next_tiles):
    R, L = lax.axis_size("row"), lax.axis_size("loop")
    g = 4 if R % 4 == 0 else R
    gr = g
    Z, G = R // gr, gr * L
    T = masks.shape[1]
    PR, K = panels.shape
    rows = right_side.shape[0]
    U = rows // T
    entries = masks.shape[0]
    per_panel = entries // L
    assert per_panel < 1 << COUNT_BITS and U * COUNT_BITS <= 32
    sizes = (R, L, g, gr, T, U, K, PR, per_panel)
    hbm = pl.BlockSpec(memory_space=pl.ANY)
    smem = pl.BlockSpec(memory_space=pltpu.SMEM)
    vmem = pl.BlockSpec(memory_space=pltpu.VMEM)
    field = jax.ShapeDtypeStruct((rows, K), F32)
    dma = pltpu.SemaphoreType.DMA
    q, p, coef = pl.pallas_call(
        functools.partial(kernel, sizes),
        out_shape=(field, field, jax.ShapeDtypeStruct((8, 128), F32)),
        in_specs=[smem, smem] + [hbm] * 5,
        out_specs=(hbm, hbm, vmem),
        scratch_shapes=[
            pltpu.VMEM((rows, K), F32),
            pltpu.VMEM((rows, K), F32),
            pltpu.VMEM((rows, K), F32),
            pltpu.VMEM((rows, K), BF16),
            pltpu.VMEM((rows, K), BF16),
            pltpu.VMEM((L, PR, K), F32),
            pltpu.VMEM((L, PR, K), BF16),
            pltpu.VMEM((L, PR, K), BF16),
            pltpu.VMEM((entries, T, T), jnp.int32),
            pltpu.VMEM((L, T, PR), jnp.int32),
            pltpu.VMEM((rows, T), F32),
            pltpu.VMEM((rows, T), F32),
            pltpu.VMEM((U, T, 3 * T), BF16),
            pltpu.VMEM((U, T, 3 * T), BF16),
            pltpu.VMEM((rows, T), F32),
            pltpu.VMEM((2, T, K), F32),
            pltpu.VMEM((2, T, K), F32),
            pltpu.VMEM((2, T, K), F32),
            pltpu.VMEM((T, T), F32),
            pltpu.VMEM((1, 8, 128), F32),
            pltpu.VMEM((1, G, 8, 128), F32),
            pltpu.VMEM((1, 8, 128), F32),
            pltpu.VMEM((1, Z, 8, 128), F32),
            dma((7,)),
            dma((L,)),
            dma((L,)),
            dma((L, g)),
            dma((L, g)),
            dma((2, 3)),
            dma((2, 3)),
            dma((1, G)),
            dma((1, G)),
            dma((1, Z)),
            dma((1, Z)),
        ],
        compiler_params=pltpu.CompilerParams(
            collective_id=0, has_side_effects=True, vmem_limit_bytes=60 * 1024 * 1024
        ),
        cost_estimate=pl.CostEstimate(flops=8 * rows * K * PR * L, bytes_accessed=8 * rows * K * 4, transcendentals=0),
    )(block_users, block_items, panels, right_side, masks, self_tiles, next_tiles)
    steps = 2
    block = pl.BlockSpec((rows // steps, K), lambda i: (i, 0))
    return pl.pallas_call(
        finish,
        grid=(steps,),
        out_shape=(field, field),
        in_specs=[pl.BlockSpec((8, 128), lambda i: (0, 0)), block, block, block],
        out_specs=(block, block),
    )(coef, right_side, q, p)


def solution(mesh):
    placed = (
        P("loop", None),
        P(("row", "loop"), None),
        P(("row", "loop")),
        P(("row", "loop")),
        P(("row", "loop"), None, None),
        P(("row", "loop"), None),
        P(("row", "loop"), None),
    )
    return jax.shard_map(
        body,
        mesh=mesh,
        in_specs=placed,
        out_specs=(P(("row", "loop"), None), P(("row", "loop"), None)),
        check_vma=False,
    )
```
